32 devices in a mesh: row: 8 (over y, x, core), col: 4 (over z).
Axes of the slice: x: 2, y: 2, z: 4, core: 2. Of those that a mesh axis runs over, the one named last changes fastest.
Arguments:
- tiles: bfloat16 [8, 4, 80, 256, 256], P('row', 'col'), may hold values from -0.125 to 0.125
- tile_coords: int32 [2, 8, 4, 80], P(None, 'row', 'col'), may hold values from 0 to 1023, as said below
- tile_counts: int32 [8, 4], P('row', 'col'), may hold values from 40 to 80, as said below
- vectors: bfloat16 [262144, 16], P(('row', 'col')), may hold values from -6 to 6
Outputs:
- product: float32 [262144, 16], P(('row', 'col'))
The draws below stay inside these ranges and needn't reach their ends.
Inputs may be any that keep to these rules, and one draw needn't show every extreme that they name: `tile_coords`: for slot s below tile_counts[r, c]: the tile row I lies in r * 128 to (r + 1) * 128 - 1; the tile column J has (J // 32) % 4 equal to c; when I != J, I < J exactly when I + J is even; no (row, column) pair appears in two live slots anywhere. Among the live slots of one device at most 35 have tile rows in any one run of 32 tile rows, and at most 28 have tile columns in any one run of 32 tile columns; a device with all slots live reaches both. Slots at or above the count hold 0. `tile_counts`: some device holds exactly 80 live slots.
All inputs are finite; a program needn't handle non-finite values.
Results may differ from the reference program's by a relative error of at most 0.0075.
Values may be sent and summed in bfloat16 or wider, within the bound.
A program may use at most 320 MiB of HBM per device.

```python
import jax
import jax.numpy as jnp
from jax import lax

TILE = 256
VECS = 16
TPS = 32
TILES_DEV = 80
ORDER = 262144
N_ROW = 8
N_COL = 4


def owner_draw(sub_key, owners, dev_total):
    hot_slots = TILES_DEV // 4
    rounds = (TILES_DEV - hot_slots + owners - 1) // owners
    slot_ids = jnp.arange(TILES_DEV, dtype=jnp.int32)
    busiest = jax.random.randint(jax.random.fold_in(sub_key, 1), (dev_total,), 0, owners).astype(jnp.int32)
    scores = jax.random.randint(jax.random.fold_in(sub_key, 2), (dev_total, rounds, owners - 1), 0, 2 ** 20) * owners
    scores = scores + jnp.arange(owners - 1, dtype=jnp.int32)[None, None, :]
    orders = jnp.argsort(scores, axis=-1).astype(jnp.int32)
    others = orders + (orders >= busiest[:, None, None]).astype(jnp.int32)
    offset = jnp.maximum(slot_ids - hot_slots, 0)
    round_ids = offset // owners
    position = offset % owners
    picked = others[:, round_ids, jnp.maximum(position - 1, 0)]
    return jnp.where((position == 0)[None, :], busiest[:, None], picked).astype(jnp.int32)


def pattern_draw(key):
    key = jax.random.fold_in(key, 7)
    dev_total = N_ROW * N_COL
    row_span = TPS * N_COL
    half_cells = TPS * TPS // 2
    half_side = TPS // 2
    device_ids = jnp.arange(dev_total, dtype=jnp.int32)
    row_here = device_ids // N_COL
    col_here = device_ids % N_COL
    slot_ids = jnp.arange(TILES_DEV, dtype=jnp.int32)
    row_owner = owner_draw(jax.random.fold_in(key, 10), N_COL, dev_total)
    col_owner = owner_draw(jax.random.fold_in(key, 20), N_ROW, dev_total)
    earlier = (slot_ids[None, :] < slot_ids[:, None])[None]
    same_block = (row_owner[:, :, None] == row_owner[:, None, :]) & (col_owner[:, :, None] == col_owner[:, None, :]) & earlier
    rank = jnp.sum(same_block.astype(jnp.int32), axis=2)
    offsets = jax.random.randint(jax.random.fold_in(key, 3), (dev_total, N_COL, N_ROW), 0, half_cells).astype(jnp.int32)
    block_off = offsets[device_ids[:, None], row_owner, col_owner]
    cell_scores = jax.random.randint(jax.random.fold_in(key, 4), (dev_total, half_cells), 0, 2 ** 20) * half_cells
    cell_scores = cell_scores + jnp.arange(half_cells, dtype=jnp.int32)[None, :]
    cell_perm = jnp.argsort(cell_scores, axis=1).astype(jnp.int32)
    cells = jnp.take_along_axis(cell_perm, (rank + block_off) % half_cells, axis=1)
    inner_row = cells // half_side
    inner_pair = cells % half_side
    pick_rows = row_here[:, None] * row_span + row_owner * TPS + inner_row
    col_first = (col_owner * N_COL + col_here[:, None]) * TPS + 2 * inner_pair
    kept = (pick_rows == col_first) | ((pick_rows < col_first) == ((pick_rows + col_first) % 2 == 0))
    pick_cols = jnp.where(kept, col_first, col_first + 1)
    drawn = jax.random.randint(jax.random.fold_in(key, 5), (dev_total,), TILES_DEV // 2, TILES_DEV + 1)
    full_dev = jax.random.randint(jax.random.fold_in(key, 6), (), 0, dev_total)
    counts = jnp.where(device_ids == full_dev, TILES_DEV, drawn).astype(jnp.int32)
    live_slots = slot_ids[None, :] < counts[:, None]
    pick_rows = jnp.where(live_slots, pick_rows, 0).astype(jnp.int32)
    pick_cols = jnp.where(live_slots, pick_cols, 0).astype(jnp.int32)
    return (pick_rows, pick_cols, counts)


def draw_tile_coords(key, part):
    pick_rows, pick_cols, _ = pattern_draw(key)
    return jnp.stack([pick_rows, pick_cols]).reshape(2, N_ROW, N_COL, TILES_DEV)


def draw_tile_counts(key, part):
    _, _, counts = pattern_draw(key)
    return counts.reshape(N_ROW, N_COL)


def levels(rng, extent, pieces, low, largest):
    loudness, own = 1.0, jax.random.fold_in(rng, 6)
    for dim, blocks in pieces:
        steps = jnp.exp(jax.random.uniform(jax.random.fold_in(own, dim), (blocks,), jnp.float32, low / len(pieces), largest / len(pieces)))
        loudness = loudness * jnp.repeat(steps, extent[dim] // blocks).reshape([-1 if axis == dim else 1 for axis in range(len(extent))])
    return loudness


def gaussian(rng, extent, deviation, reach, cuts=(), kind=jnp.bfloat16):
    result = jax.random.normal(rng, extent, jnp.float32) * deviation
    if len(cuts) > 0:
        result = levels(rng, extent, cuts, -0.22, 0.18) * result
    return jnp.clip(result, min=-reach, max=reach).astype(kind)


def setup_inputs(seed: int = 0) -> dict:
    keys = jax.random.split(jax.random.key(seed), 5)
    return {
        "tiles": gaussian(keys[0], (N_ROW, N_COL, TILES_DEV, TILE, TILE), (8 * TILE) ** -0.5, 0.125, ((0, 8), (1, 4))),
        "tile_coords": draw_tile_coords(jax.random.fold_in(keys[4], 71), 0),
        "tile_counts": draw_tile_counts(jax.random.fold_in(keys[4], 71), 0),
        "vectors": gaussian(keys[3], (ORDER, VECS), 1.0, 6.0, ((0, 32),)),
    }


def split_tile(stored, tile_rows, tile_cols):
    size_tile = stored.shape[-1]
    down_idx = jnp.arange(size_tile, dtype=jnp.int32)[:, None]
    across_idx = jnp.arange(size_tile, dtype=jnp.int32)[None, :]
    off_diag = (tile_rows != tile_cols)[:, None, None]
    zero_val = jnp.zeros((), stored.dtype)
    upper_part = jnp.where(off_diag | (down_idx <= across_idx)[None], stored, zero_val)
    lower_part = jnp.where(off_diag | (down_idx < across_idx)[None], stored, zero_val)
    return upper_part, lower_part


def reference(tiles, tile_coords, tile_counts, vectors):
    dev_total = N_ROW * N_COL
    slot_count = tiles.shape[2]
    size_tile = tiles.shape[-1]
    vector_width = vectors.shape[1]
    vec_tiles = vectors.reshape(-1, size_tile, vector_width)
    flat_tiles = tiles.reshape(dev_total, slot_count, size_tile, size_tile)
    flat_rows = tile_coords[0].reshape(dev_total, slot_count).astype(jnp.int32)
    flat_cols = tile_coords[1].reshape(dev_total, slot_count).astype(jnp.int32)
    flat_counts = tile_counts.reshape(dev_total).astype(jnp.int32)

    def one_device(running, device_item):
        stored, tile_rows, tile_cols, live_count = device_item
        live_slots = jnp.arange(slot_count, dtype=jnp.int32) < live_count
        upper_part, lower_part = split_tile(stored, tile_rows, tile_cols)
        col_vecs = vec_tiles[tile_cols].astype(jnp.float32)
        row_vecs = vec_tiles[tile_rows].astype(jnp.float32)
        apply_operator = jnp.einsum("tab,tbv->tav", upper_part.astype(jnp.float32), col_vecs).astype(jnp.bfloat16)
        mirror = jnp.einsum("tba,tbv->tav", lower_part.astype(jnp.float32), row_vecs).astype(jnp.bfloat16)
        apply_operator = jnp.where(live_slots[:, None, None], apply_operator.astype(jnp.float32), jnp.float32(0.0))
        mirror = jnp.where(live_slots[:, None, None], mirror.astype(jnp.float32), jnp.float32(0.0))
        running = running.at[tile_rows].add(apply_operator)
        running = running.at[tile_cols].add(mirror)
        return running, None

    start_sum = jnp.zeros(vec_tiles.shape, jnp.float32)
    running, _ = lax.scan(one_device, start_sum, (flat_tiles, flat_rows, flat_cols, flat_counts))
    return running.reshape(-1, vector_width)
```

```python
import functools

import jax
import jax.numpy as jnp
from jax import lax
from jax.experimental import pallas as pl
from jax.experimental.pallas import tpu as pltpu
from jax.sharding import PartitionSpec as P

MESH = pl.DeviceIdType.MESH
VMEM_LIMIT = 48 * 1024 * 1024
GROUP = 8


def gather_kernel(
    x_ref, xr_ref, xc_ref, own_sem, zs, zr, cs, cr, ss, sr, fs, fr
):
    r, c = lax.axis_index("row"), lax.axis_index("col")
    chip, core = r // 2, r % 2
    sib = 2 * chip + 1 - core

    barrier = pltpu.get_barrier_semaphore()
    for d in range(1, 4):
        pl.semaphore_signal(barrier, inc=1, device_id=(r, (c + d) % 4), device_id_type=MESH)
        pl.semaphore_signal(
            barrier, inc=1, device_id=(2 * ((chip + d) % 4) + core, c), device_id_type=MESH
        )
    pl.semaphore_signal(barrier, inc=1, device_id=(sib, c), device_id_type=MESH)
    pl.semaphore_wait(barrier, 7)

    def z_copy(d, slot):
        return pltpu.make_async_remote_copy(
            x_ref, xr_ref.at[slot], zs.at[d], zr.at[d],
            device_id=(r, (c + d) % 4), device_id_type=MESH,
        )

    def chip_copy(d, slot):
        return pltpu.make_async_remote_copy(
            x_ref, xc_ref.at[slot], cs.at[d], cr.at[d],
            device_id=(2 * ((chip + d) % 4) + core, c), device_id_type=MESH,
        )

    def sib_copy(slot):
        return pltpu.make_async_remote_copy(
            x_ref, xc_ref.at[slot], ss, sr, device_id=(sib, c), device_id_type=MESH
        )

    def fwd_copy(d, slot):
        return pltpu.make_async_remote_copy(
            xc_ref.at[slot], xc_ref.at[slot], fs.at[d], fr.at[d],
            device_id=(sib, c), device_id_type=MESH,
        )

    for d in (2, 1, 3):
        z_copy(d, c).start()
        chip_copy(d, r).start()
    sib_copy(r).start()
    own_r = pltpu.make_async_copy(x_ref, xr_ref.at[c], own_sem.at[0])
    own_c = pltpu.make_async_copy(x_ref, xc_ref.at[r], own_sem.at[1])
    own_r.start()
    own_c.start()
    for d in (2, 1, 3):
        slot = 2 * ((chip + 4 - d) % 4) + core
        chip_copy(d, slot).wait_recv()
        fwd_copy(d, slot).start()
    sib_copy(sib).wait_recv()
    own_r.wait()
    own_c.wait()
    for d in (2, 1, 3):
        fwd_copy(d, 2 * ((chip + 4 - d) % 4) + 1 - core).wait_recv()
        z_copy(d, (c + 4 - d) % 4).wait_recv()
    for d in (2, 1, 3):
        z_copy(d, c).wait_send()
        chip_copy(d, r).wait_send()
        fwd_copy(d, 2 * ((chip + 4 - d) % 4) + core).wait_send()
    sib_copy(r).wait_send()


def gather(x):
    rows, cols = 8, 4
    dma = pltpu.SemaphoreType.DMA
    return pl.pallas_call(
        gather_kernel,
        out_shape=(
            jax.ShapeDtypeStruct((cols, *x.shape), x.dtype),
            jax.ShapeDtypeStruct((rows, *x.shape), x.dtype),
        ),
        in_specs=[pl.BlockSpec(memory_space=pl.ANY)],
        out_specs=(pl.BlockSpec(memory_space=pl.ANY),) * 2,
        scratch_shapes=[
            dma((2,)), dma((4,)), dma((4,)), dma((4,)), dma((4,)), dma, dma, dma((4,)), dma((4,)),
        ],
        compiler_params=pltpu.CompilerParams(collective_id=0, has_side_effects=True),
        name="gather_vectors",
    )(x)


def apply_kernel(
    slots, tile, per_slab, n_cols, coords, count,
    t_ref, xr_ref, xc_ref, f_ref, m_ref, facc, macc,
):
    step = pl.program_id(0)
    group = t_ref.shape[2]

    @pl.when(step == 0)
    def _():
        facc[...] = jnp.zeros_like(facc)
        macc[...] = jnp.zeros_like(macc)

    def place(s):
        tile_row, tile_col = coords[s], coords[slots + s]
        local = tile_row % (per_slab * n_cols)
        row_at = (local // per_slab, pl.multiple_of(local % per_slab * tile, tile))
        col_at = (
            tile_col // (per_slab * n_cols), pl.multiple_of(tile_col % per_slab * tile, tile),
        )
        return row_at, col_at

    def run(masked):
        made = []
        for g in range(group):
            s = step * group + g
            (ro, rp), (co, cp) = place(s)
            x_row = xr_ref[ro, :, pl.ds(rp, tile)]
            x_col = xc_ref[co, :, pl.ds(cp, tile)]
            upper = lower = t_ref[0, 0, g]
            if masked:
                off = coords[s] != coords[slots + s]
                down = lax.broadcasted_iota(jnp.int32, (tile, tile), 0)
                down = jnp.where(off, -1, down)
                across = lax.broadcasted_iota(jnp.int32, (tile, tile), 1)
                stored = upper.astype(jnp.float32)
                upper = jnp.where(down <= across, stored, 0.0).astype(jnp.bfloat16)
                lower = jnp.where(down < across, stored, 0.0).astype(jnp.bfloat16)
            forward = lax.dot_general(
                x_col, upper, (((1,), (1,)), ((), ())), preferred_element_type=jnp.float32
            )
            mirror = lax.dot_general(
                x_row, lower, (((1,), (0,)), ((), ())), preferred_element_type=jnp.float32
            )
            if masked:
                live = s < count[0]
                forward = jnp.where(live, forward, 0.0)
                mirror = jnp.where(live, mirror, 0.0)
            made.append((forward, mirror))
        for g in range(group):
            (ro, rp), (co, cp) = place(step * group + g)
            forward, mirror = made[g]
            facc[ro, :, pl.ds(rp, tile)] += forward
            macc[co, :, pl.ds(cp, tile)] += mirror

    special = coords[step * group] == coords[slots + step * group]
    for g in range(1, group):
        s = step * group + g
        special = special | (coords[s] == coords[slots + s])
    special = special | (step * group + group > count[0])

    @pl.when(special)
    def _():
        run(True)

    @pl.when(jnp.logical_not(special))
    def _():
        run(False)

    @pl.when(step == pl.num_programs(0) - 1)
    def _():
        f_ref[...] = facc[...].astype(f_ref.dtype)
        m_ref[...] = macc[...].astype(m_ref.dtype)


def apply_tiles(tiles, coords, count, xr, xc, tile):
    slots = tiles.shape[2]
    group = GROUP if slots % GROUP == 0 else 1
    n_cols = xr.shape[0]
    per_slab = xr.shape[2] // tile
    whole = lambda a: pl.BlockSpec(a.shape, lambda i, *_: (0, 0, 0))
    return pl.pallas_call(
        functools.partial(apply_kernel, slots, tile, per_slab, n_cols),
        out_shape=(
            jax.ShapeDtypeStruct(xr.shape, jnp.bfloat16),
            jax.ShapeDtypeStruct(xc.shape, jnp.bfloat16),
        ),
        grid_spec=pltpu.PrefetchScalarGridSpec(
            num_scalar_prefetch=2,
            grid=(slots // group,),
            in_specs=[
                pl.BlockSpec((1, 1, group, tile, tile), lambda i, *_: (0, 0, i, 0, 0)),
                whole(xr),
                whole(xc),
            ],
            out_specs=(whole(xr), whole(xc)),
            scratch_shapes=[
                pltpu.VMEM(xr.shape, jnp.float32),
                pltpu.VMEM(xc.shape, jnp.float32),
            ],
        ),
        compiler_params=pltpu.CompilerParams(vmem_limit_bytes=VMEM_LIMIT),
        name="apply_tiles",
    )(coords, count, tiles, xr, xc)


def scatter_kernel(
    f_ref, m_ref, o_ref, from_sib, chip_out, chip_in, r_out, r_in, l_out, l_in,
    bs, br, cs, cr, rs, rr, ls, lr,
):
    r, c = lax.axis_index("row"), lax.axis_index("col")
    chip, core = r // 2, r % 2
    sib = 2 * chip + 1 - core
    width = o_ref.shape[1]
    piece = width // 8
    f32 = jnp.float32

    barrier = pltpu.get_barrier_semaphore()
    for d in range(1, 4):
        pl.semaphore_signal(
            barrier, inc=1, device_id=(2 * ((chip + d) % 4) + core, c), device_id_type=MESH
        )
    pl.semaphore_signal(barrier, inc=1, device_id=(sib, c), device_id_type=MESH)

    @pl.when(c > 0)
    def _():
        pl.semaphore_signal(barrier, inc=1, device_id=(r, c - 1), device_id_type=MESH)

    @pl.when(c < 3)
    def _():
        pl.semaphore_signal(barrier, inc=1, device_id=(r, c + 1), device_id_type=MESH)

    ends = (c == 0) | (c == 3)

    @pl.when(ends)
    def _():
        pl.semaphore_wait(barrier, 5)

    @pl.when(jnp.logical_not(ends))
    def _():
        pl.semaphore_wait(barrier, 6)

    def right(d, src):
        return pltpu.make_async_remote_copy(
            src, r_in.at[d], rs.at[d], rr.at[d], device_id=(r, c + 1), device_id_type=MESH
        )

    def left(d, src):
        return pltpu.make_async_remote_copy(
            src, l_in.at[d], ls.at[d], lr.at[d], device_id=(r, c - 1), device_id_type=MESH
        )

    def to_sib(d):
        return pltpu.make_async_remote_copy(
            m_ref.at[2 * ((chip + d) % 4) + 1 - core], from_sib.at[d], bs.at[d], br.at[d],
            device_id=(sib, c), device_id_type=MESH,
        )

    def to_chip(d):
        return pltpu.make_async_remote_copy(
            chip_out.at[d], chip_in.at[d], cs.at[d], cr.at[d],
            device_id=(2 * ((chip + d) % 4) + core, c), device_id_type=MESH,
        )

    def add(dst, a, b):
        def body(i, _):
            at = pl.ds(pl.multiple_of(i * piece, piece), piece)
            dst[:, at] = (a[:, at].astype(f32) + b[:, at].astype(f32)).astype(dst.dtype)
            return 0

        lax.fori_loop(0, 8, body, 0)

    for i in range(3):

        @pl.when(c == 0)
        def _():
            right(3 - i, f_ref.at[3 - i]).start()

        @pl.when(c == 3)
        def _():
            left(i, f_ref.at[i]).start()

    for d in (2, 1, 3, 0):
        to_sib(d).start()
    for d in (2, 1, 3):
        to_sib(d).wait_recv()
        add(chip_out.at[d], m_ref.at[2 * ((chip + d) % 4) + core], from_sib.at[d])
        to_chip(d).start()

    for i in range(2):
        d = 3 - i

        @pl.when((c > 0) & (c < d))
        def _():
            right(d, r_out.at[d]).wait_recv()
            add(r_out.at[d], f_ref.at[d], r_in.at[d])
            right(d, r_out.at[d]).start()

        e = i

        @pl.when((c < 3) & (c > e))
        def _():
            left(e, l_out.at[e]).wait_recv()
            add(l_out.at[e], f_ref.at[e], l_in.at[e])
            left(e, l_out.at[e]).start()

    to_sib(0).wait_recv()
    for d in (2, 1, 3):
        to_chip(d).wait_recv()

    def first(i, _):
        at = pl.ds(pl.multiple_of(i * piece, piece), piece)
        total = f_ref[c, :, at].astype(f32) + m_ref[r, :, at].astype(f32)
        total = total + from_sib[0, :, at].astype(f32)
        for d in (2, 1, 3):
            total = total + chip_in[d, :, at].astype(f32)
        o_ref[:, at] = total
        return 0

    lax.fori_loop(0, 8, first, 0)

    @pl.when(c > 0)
    def _():
        right(c, r_out.at[c]).wait_recv()
        add(o_ref, o_ref, r_in.at[c])

    @pl.when(c < 3)
    def _():
        left(c, l_out.at[c]).wait_recv()
        add(o_ref, o_ref, l_in.at[c])

    for d in range(4):
        to_sib(d).wait_send()
    for d in (2, 1, 3):
        to_chip(d).wait_send()
    for i in range(3):

        @pl.when(c < 3 - i)
        def _():
            right(3 - i, r_out.at[3 - i]).wait_send()

        @pl.when(c > i)
        def _():
            left(i, l_out.at[i]).wait_send()


def scatter(f, m):
    dma = pltpu.SemaphoreType.DMA
    block = pltpu.VMEM((4, *f.shape[1:]), f.dtype)
    return pl.pallas_call(
        scatter_kernel,
        out_shape=jax.ShapeDtypeStruct(f.shape[1:], jnp.float32),
        in_specs=[pl.BlockSpec(memory_space=pltpu.VMEM)] * 2,
        out_specs=pl.BlockSpec(memory_space=pltpu.VMEM),
        scratch_shapes=[block] * 7 + [dma((4,))] * 8,
        compiler_params=pltpu.CompilerParams(
            collective_id=1, has_side_effects=True, vmem_limit_bytes=VMEM_LIMIT
        ),
        name="scatter_products",
    )(f, m)


def shards(n_rows, n_cols, tiles, tile_coords, tile_counts, vectors):
    tile = tiles.shape[-1]
    x = vectors.T
    coords, count = tile_coords.reshape(-1), tile_counts.reshape(-1)
    direct = (n_rows, n_cols) == (8, 4)
    if direct:
        xr, xc = gather(x)
    else:
        xr = lax.all_gather(x, "col", axis=0)
        xc = lax.all_gather(x, "row", axis=0)
    f, m = apply_tiles(tiles, coords, count, xr, xc, tile)
    if direct:
        product = scatter(f, m)
    else:
        f = lax.all_to_all(f, "col", 0, 0, tiled=True)
        m = lax.all_to_all(m, "row", 0, 0, tiled=True)
        product = jnp.sum(f.astype(jnp.float32), 0) + jnp.sum(m.astype(jnp.float32), 0)
    return product.T


def solution(mesh):
    in_specs = (
        P("row", "col", None, None, None),
        P(None, "row", "col", None),
        P("row", "col"),
        P(("row", "col"), None),
    )
    out_specs = P(("row", "col"), None)
    body = functools.partial(shards, mesh.shape["row"], mesh.shape["col"])
    return jax.shard_map(body, mesh=mesh, in_specs=in_specs, out_specs=out_specs, check_vma=False)
```

```python
import functools

import jax
import jax.numpy as jnp
from jax import lax
from jax.experimental import pallas as pl
from jax.experimental.pallas import tpu as pltpu
from jax.sharding import PartitionSpec as P

MESH = pl.DeviceIdType.MESH
VMEM_LIMIT = 48 * 1024 * 1024
GROUP = 8


def fused_kernel(
    coords, count, coords_v, x_ref, t_ref, o_ref,
    mine, xr, xc, upper, lower, tri, made, keys, onehot, f_ref, m_ref,
    from_sib, chip_out, chip_in, r_out, r_in, l_out, l_in,
    tile_sem, own_sem, zs, zr, gs, gr, ss, sr, fs, fr, bs, br, cs, cr, rs, rr, ls, lr,
):
    r, c = lax.axis_index("row"), lax.axis_index("col")
    chip, core = r // 2, r % 2
    sib = 2 * chip + 1 - core
    slots, tile = upper.shape[0], upper.shape[1]
    vecs, width = x_ref.shape
    per_slab = width // tile
    groups = slots // GROUP
    f32, bf16, i32 = jnp.float32, jnp.bfloat16, jnp.int32

    for p in range(per_slab):
        mine[p] = x_ref[:, p * tile : (p + 1) * tile]

    def slab(i):
        return pl.ds(i * per_slab, per_slab)

    def chip_at(d):
        return (chip + d) % 4

    def tile_copy(g):
        at = pl.ds(g * GROUP, GROUP)
        return pltpu.make_async_copy(t_ref.at[0, 0, at], lower.at[at], tile_sem.at[g])

    barrier = pltpu.get_barrier_semaphore()
    for d in range(1, 4):
        pl.semaphore_signal(barrier, inc=1, device_id=(r, (c + d) % 4), device_id_type=MESH)
        pl.semaphore_signal(
            barrier, inc=1, device_id=(2 * chip_at(d) + core, c), device_id_type=MESH
        )
    pl.semaphore_signal(barrier, inc=1, device_id=(sib, c), device_id_type=MESH)
    pl.semaphore_wait(barrier, 7)

    def remote(src, dst, send, recv, row, col):
        return pltpu.make_async_remote_copy(
            src, dst, send, recv, device_id=(row, col), device_id_type=MESH
        )

    def z_copy(d, slot):
        return remote(mine, xr.at[slab(slot)], zs.at[d], zr.at[d], r, (c + d) % 4)

    def chip_copy(d, slot):
        return remote(mine, xc.at[slab(slot)], gs.at[d], gr.at[d], 2 * chip_at(d) + core, c)

    def sib_copy(slot):
        return remote(mine, xc.at[slab(slot)], ss, sr, sib, c)

    def fwd_copy(d, slot):
        return remote(xc.at[slab(slot)], xc.at[slab(slot)], fs.at[d], fr.at[d], sib, c)

    def right(d, src):
        return remote(src, r_in.at[d], rs.at[d], rr.at[d], r, c + 1)

    def left(d, src):
        return remote(src, l_in.at[d], ls.at[d], lr.at[d], r, c - 1)

    def to_sib(d):
        return remote(
            m_ref.at[2 * chip_at(d) + 1 - core], from_sib.at[d], bs.at[d], br.at[d], sib, c
        )

    def to_chip(d):
        return remote(
            chip_out.at[d], chip_in.at[d], cs.at[d], cr.at[d], 2 * chip_at(d) + core, c
        )

    for d in (2, 1, 3):
        chip_copy(d, r).start()
        z_copy(d, c).start()
    sib_copy(r).start()
    own_r = pltpu.make_async_copy(mine, xr.at[slab(c)], own_sem.at[0])
    own_c = pltpu.make_async_copy(mine, xc.at[slab(r)], own_sem.at[1])
    own_r.start()
    own_c.start()

    def start_tiles(g, _):
        tile_copy(g).start()
        return 0

    lax.fori_loop(0, groups, start_tiles, 0)

    tile_row, tile_col = coords_v[0, 0], coords_v[1, 0]
    live = lax.broadcasted_iota(i32, (1, slots), 1) < count[0, 0]
    span = 4 * per_slab
    places = (tile_row % span, tile_col // span * per_slab + tile_col % per_slab)
    wide = slots * vecs
    spread = lax.broadcasted_iota(i32, (slots, wide), 1) // vecs
    spread = (spread == lax.broadcasted_iota(i32, (slots, wide), 0)).astype(f32).astype(bf16)
    across = lax.broadcasted_iota(i32, (vecs, wide), 1) % vecs
    same = across == lax.broadcasted_iota(i32, (vecs, wide), 0)
    for k in range(2):
        place = jnp.where(live, places[k], -1).astype(f32)
        place = jnp.broadcast_to(place, (vecs, slots)).astype(bf16)
        place = jnp.dot(place, spread, preferred_element_type=f32)
        keys[k] = jnp.where(same, place, -1.0)

    down = lax.broadcasted_iota(i32, (tile, tile), 0)
    over = lax.broadcasted_iota(i32, (tile, tile), 1)
    tri[0] = (down <= over).astype(f32).astype(bf16)
    tri[1] = (down < over).astype(f32).astype(bf16)

    def split_group(g, _):
        tile_copy(g).wait()
        for i in range(GROUP):
            s = g * GROUP + i
            gap = jnp.full((1, tile), coords[0, 0, 0, s] - coords[1, 0, 0, s], i32)
            off = jnp.minimum(gap * gap, 1).astype(f32).astype(bf16)
            stored = lower[s]
            upper[s] = stored * jnp.maximum(tri[0], off)
            lower[s] = stored * jnp.maximum(tri[1], off)
        return 0

    lax.fori_loop(0, groups, split_group, 0)

    for d in (2, 1, 3):
        slot = 2 * ((chip + 4 - d) % 4) + core
        chip_copy(d, slot).wait_recv()
        fwd_copy(d, slot).start()
    sib_copy(sib).wait_recv()
    own_c.wait()
    for d in (2, 1, 3):
        fwd_copy(d, 2 * ((chip + 4 - d) % 4) + 1 - core).wait_recv()

    def forward_group(g, _):
        outs = []
        for i in range(GROUP):
            s = g * GROUP + i
            col = coords[1, 0, 0, s]
            at = lax.div(col, span) * per_slab + lax.rem(col, per_slab)
            outs.append(
                lax.dot_general(
                    xc[at], upper[s], (((1,), (1,)), ((), ())),
                    preferred_element_type=f32,
                ).astype(bf16)
            )
        rows = pl.ds(pl.multiple_of(g * GROUP * vecs, GROUP * vecs), GROUP * vecs)
        made[rows, :] = jnp.concatenate(outs, axis=0)
        return 0

    def mirror_group(g, _):
        outs = []
        for i in range(GROUP):
            s = g * GROUP + i
            row = lax.rem(coords[0, 0, 0, s], span)
            outs.append(
                jnp.dot(xr[row], lower[s], preferred_element_type=f32).astype(bf16)
            )
        rows = pl.ds(pl.multiple_of(g * GROUP * vecs, GROUP * vecs), GROUP * vecs)
        made[rows, :] = jnp.concatenate(outs, axis=0)
        return 0

    def combine(k, owner, dst):
        def pick(p, _):
            rows = pl.ds(pl.multiple_of(p * vecs, vecs), vecs)
            wanted = (owner * per_slab + p).astype(f32)
            onehot[rows, :] = jnp.where(keys[k] == wanted, 1.0, 0.0).astype(bf16)
            return 0

        lax.fori_loop(0, per_slab, pick, 0, unroll=4)
        dst[owner] = jnp.dot(onehot[...], made[...], preferred_element_type=f32).astype(bf16)

    def add(dst, a, b):
        dst[...] = (a[...].astype(f32) + b[...].astype(f32)).astype(dst.dtype)

    def chain(i):
        d, e = 3 - i, i

        @pl.when((c > 0) & (c < d))
        def _():
            right(d, r_out.at[d]).wait_recv()
            add(r_out.at[d], f_ref.at[d], r_in.at[d])
            right(d, r_out.at[d]).start()

        @pl.when((c < 3) & (c > e))
        def _():
            left(e, l_out.at[e]).wait_recv()
            add(l_out.at[e], f_ref.at[e], l_in.at[e])
            left(e, l_out.at[e]).start()

    lax.fori_loop(0, groups, forward_group, 0)

    def combine_f(d, _):
        combine(0, d, f_ref)
        return 0

    lax.fori_loop(0, 4, combine_f, 0)
    for i in range(3):

        @pl.when(c == 0)
        def _():
            right(3 - i, f_ref.at[3 - i]).start()

        @pl.when(c == 3)
        def _():
            left(i, f_ref.at[i]).start()

    own_r.wait()
    for d in (2, 1, 3):
        z_copy(d, (c + 4 - d) % 4).wait_recv()
    lax.fori_loop(0, groups, mirror_group, 0)
    chain(0)

    def combine_theirs(j, _):
        combine(1, 2 * ((chip + 1 + j) % 4) + 1 - core, m_ref)
        to_sib((1 + j) % 4).start()
        return 0

    lax.fori_loop(0, 4, combine_theirs, 0)

    def combine_ours(j, _):
        combine(1, 2 * ((chip + 1 + j) % 4) + core, m_ref)
        return 0

    lax.fori_loop(0, 4, combine_ours, 0)
    for d in (1, 2, 3):
        to_sib(d).wait_recv()
        add(chip_out.at[d], m_ref.at[2 * chip_at(d) + core], from_sib.at[d])
        to_chip(d).start()
    chain(1)
    to_sib(0).wait_recv()
    for d in (1, 2, 3):
        to_chip(d).wait_recv()

    def rows_of(p):
        rows = pl.ds(pl.multiple_of(p * vecs, vecs), vecs)
        return rows, pl.ds(pl.multiple_of(p * tile, tile), tile)

    def total(p, _):
        rows, at = rows_of(p)
        out = f_ref[c, rows, :].astype(f32) + m_ref[r, rows, :].astype(f32)
        out = out + from_sib[0, rows, :].astype(f32)
        for d in (1, 2, 3):
            out = out + chip_in[d, rows, :].astype(f32)
        o_ref[:, at] = out
        return 0

    lax.fori_loop(0, per_slab, total, 0, unroll=4)

    def last(src):
        def body(p, _):
            rows, at = rows_of(p)
            o_ref[:, at] = o_ref[:, at] + src[c, rows, :].astype(f32)
            return 0

        lax.fori_loop(0, per_slab, body, 0, unroll=4)

    @pl.when(c > 0)
    def _():
        right(c, r_out.at[c]).wait_recv()
        last(r_in)

    @pl.when(c < 3)
    def _():
        left(c, l_out.at[c]).wait_recv()
        last(l_in)

    for d in (1, 2, 3):
        z_copy(d, c).wait_send()
        chip_copy(d, r).wait_send()
        fwd_copy(d, 2 * ((chip + 4 - d) % 4) + core).wait_send()
        to_chip(d).wait_send()
    sib_copy(r).wait_send()
    for d in range(4):
        to_sib(d).wait_send()
    for i in range(3):

        @pl.when(c < 3 - i)
        def _():
            right(3 - i, r_out.at[3 - i]).wait_send()

        @pl.when(c > i)
        def _():
            left(i, l_out.at[i]).wait_send()


def fused(tiles, tile_coords, tile_counts, x):
    slots, tile = tiles.shape[2], tiles.shape[-1]
    vecs, width = x.shape
    slab = width // tile
    rows = slab * vecs
    dma, bf16 = pltpu.SemaphoreType.DMA, jnp.bfloat16
    block = pltpu.VMEM((4, rows, tile), bf16)
    return pl.pallas_call(
        fused_kernel,
        out_shape=jax.ShapeDtypeStruct(x.shape, jnp.float32),
        in_specs=[
            pl.BlockSpec(memory_space=pltpu.SMEM),
            pl.BlockSpec(memory_space=pltpu.SMEM),
            pl.BlockSpec(memory_space=pltpu.VMEM),
            pl.BlockSpec(memory_space=pltpu.VMEM),
            pl.BlockSpec(memory_space=pl.ANY),
        ],
        out_specs=pl.BlockSpec(memory_space=pltpu.VMEM),
        scratch_shapes=[
            pltpu.VMEM((slab, vecs, tile), bf16),
            pltpu.VMEM((4 * slab, vecs, tile), bf16),
            pltpu.VMEM((8 * slab, vecs, tile), bf16),
            pltpu.VMEM((slots, tile, tile), bf16),
            pltpu.VMEM((slots, tile, tile), bf16),
            pltpu.VMEM((2, tile, tile), bf16),
            pltpu.VMEM((slots * vecs, tile), bf16),
            pltpu.VMEM((2, vecs, slots * vecs), jnp.float32),
            pltpu.VMEM((rows, slots * vecs), bf16),
            block,
            pltpu.VMEM((8, rows, tile), bf16),
            *[block] * 7,
            dma((slots // GROUP,)),
            dma((2,)),
            *[dma((4,))] * 4,
            *[dma] * 2,
            *[dma((4,))] * 10,
        ],
        compiler_params=pltpu.CompilerParams(
            collective_id=0, has_side_effects=True, vmem_limit_bytes=VMEM_LIMIT
        ),
        name="fused_product",
    )(tile_coords, tile_counts, tile_coords, x, tiles)


def apply_kernel(
    slots, tile, per_slab, n_cols, coords, count,
    t_ref, xr_ref, xc_ref, f_ref, m_ref, facc, macc,
):
    step = pl.program_id(0)
    group = t_ref.shape[2]

    @pl.when(step == 0)
    def _():
        facc[...] = jnp.zeros_like(facc)
        macc[...] = jnp.zeros_like(macc)

    def place(s):
        tile_row, tile_col = coords[s], coords[slots + s]
        local = tile_row % (per_slab * n_cols)
        row_at = (local // per_slab, pl.multiple_of(local % per_slab * tile, tile))
        col_at = (
            tile_col // (per_slab * n_cols), pl.multiple_of(tile_col % per_slab * tile, tile),
        )
        return row_at, col_at

    def run(masked):
        made = []
        for g in range(group):
            s = step * group + g
            (ro, rp), (co, cp) = place(s)
            x_row = xr_ref[ro, :, pl.ds(rp, tile)]
            x_col = xc_ref[co, :, pl.ds(cp, tile)]
            upper = lower = t_ref[0, 0, g]
            if masked:
                off = coords[s] != coords[slots + s]
                down = lax.broadcasted_iota(jnp.int32, (tile, tile), 0)
                down = jnp.where(off, -1, down)
                across = lax.broadcasted_iota(jnp.int32, (tile, tile), 1)
                stored = upper.astype(jnp.float32)
                upper = jnp.where(down <= across, stored, 0.0).astype(jnp.bfloat16)
                lower = jnp.where(down < across, stored, 0.0).astype(jnp.bfloat16)
            forward = lax.dot_general(
                x_col, upper, (((1,), (1,)), ((), ())), preferred_element_type=jnp.float32
            )
            mirror = lax.dot_general(
                x_row, lower, (((1,), (0,)), ((), ())), preferred_element_type=jnp.float32
            )
            if masked:
                live = s < count[0]
                forward = jnp.where(live, forward, 0.0)
                mirror = jnp.where(live, mirror, 0.0)
            made.append((forward, mirror))
        for g in range(group):
            (ro, rp), (co, cp) = place(step * group + g)
            forward, mirror = made[g]
            facc[ro, :, pl.ds(rp, tile)] += forward
            macc[co, :, pl.ds(cp, tile)] += mirror

    special = coords[step * group] == coords[slots + step * group]
    for g in range(1, group):
        s = step * group + g
        special = special | (coords[s] == coords[slots + s])
    special = special | (step * group + group > count[0])

    @pl.when(special)
    def _():
        run(True)

    @pl.when(jnp.logical_not(special))
    def _():
        run(False)

    @pl.when(step == pl.num_programs(0) - 1)
    def _():
        f_ref[...] = facc[...].astype(f_ref.dtype)
        m_ref[...] = macc[...].astype(m_ref.dtype)


def apply_tiles(tiles, coords, count, xr, xc, tile):
    slots = tiles.shape[2]
    group = GROUP if slots % GROUP == 0 else 1
    n_cols = xr.shape[0]
    per_slab = xr.shape[2] // tile
    whole = lambda a: pl.BlockSpec(a.shape, lambda i, *_: (0, 0, 0))
    return pl.pallas_call(
        functools.partial(apply_kernel, slots, tile, per_slab, n_cols),
        out_shape=(
            jax.ShapeDtypeStruct(xr.shape, jnp.bfloat16),
            jax.ShapeDtypeStruct(xc.shape, jnp.bfloat16),
        ),
        grid_spec=pltpu.PrefetchScalarGridSpec(
            num_scalar_prefetch=2,
            grid=(slots // group,),
            in_specs=[
                pl.BlockSpec((1, 1, group, tile, tile), lambda i, *_: (0, 0, i, 0, 0)),
                whole(xr),
                whole(xc),
            ],
            out_specs=(whole(xr), whole(xc)),
            scratch_shapes=[
                pltpu.VMEM(xr.shape, jnp.float32),
                pltpu.VMEM(xc.shape, jnp.float32),
            ],
        ),
        compiler_params=pltpu.CompilerParams(vmem_limit_bytes=VMEM_LIMIT),
        name="apply_tiles",
    )(coords, count, tiles, xr, xc)


def shards(n_rows, n_cols, tiles, tile_coords, tile_counts, vectors):
    tile = tiles.shape[-1]
    x = vectors.T
    if (n_rows, n_cols) == (8, 4):
        return fused(tiles, tile_coords, tile_counts, x).T
    coords, count = tile_coords.reshape(-1), tile_counts.reshape(-1)
    xr = lax.all_gather(x, "col", axis=0)
    xc = lax.all_gather(x, "row", axis=0)
    f, m = apply_tiles(tiles, coords, count, xr, xc, tile)
    f = lax.all_to_all(f, "col", 0, 0, tiled=True)
    m = lax.all_to_all(m, "row", 0, 0, tiled=True)
    return (jnp.sum(f.astype(jnp.float32), 0) + jnp.sum(m.astype(jnp.float32), 0)).T


def solution(mesh):
    in_specs = (
        P("row", "col", None, None, None),
        P(None, "row", "col", None),
        P("row", "col"),
        P(("row", "col"), None),
    )
    out_specs = P(("row", "col"), None)
    body = functools.partial(shards, mesh.shape["row"], mesh.shape["col"])
    return jax.shard_map(body, mesh=mesh, in_specs=in_specs, out_specs=out_specs, check_vma=False)
```

```python
import functools

import jax
import jax.numpy as jnp
from jax import lax
from jax.experimental import pallas as pl
from jax.experimental.pallas import tpu as pltpu
from jax.sharding import PartitionSpec as P

MESH = pl.DeviceIdType.MESH
VMEM_LIMIT = 48 * 1024 * 1024
GROUP = 8


def fused_kernel(
    coords, count, coords_v, x_ref, t_ref, o_ref,
    mine, xr, xc, upper, lower, tri, made, keys, onehot, f_ref, m_ref,
    from_sib, chip_out, chip_in, r_out, r_in, l_out, l_in,
    tile_sem, own_sem, zs, zr, gs, gr, ss, sr, fs, fr, bs, br, cs, cr, rs, rr, ls, lr,
):
    r, c = lax.axis_index("row"), lax.axis_index("col")
    chip, core = r // 2, r % 2
    sib = 2 * chip + 1 - core
    slots, tile = upper.shape[0], upper.shape[1]
    vecs, width = x_ref.shape
    per_slab = width // tile
    groups = slots // GROUP
    f32, bf16, i32 = jnp.float32, jnp.bfloat16, jnp.int32

    for p in range(per_slab):
        mine[p] = x_ref[:, p * tile : (p + 1) * tile]

    def slab(i):
        return pl.ds(i * per_slab, per_slab)

    def chip_at(d):
        return (chip + d) % 4

    def tile_copy(g):
        at = pl.ds(g * GROUP, GROUP)
        return pltpu.make_async_copy(t_ref.at[0, 0, at], lower.at[at], tile_sem.at[g])

    barrier = pltpu.get_barrier_semaphore()
    for d in range(1, 4):
        pl.semaphore_signal(barrier, inc=1, device_id=(r, (c + d) % 4), device_id_type=MESH)
        pl.semaphore_signal(
            barrier, inc=1, device_id=(2 * chip_at(d) + core, c), device_id_type=MESH
        )
    pl.semaphore_signal(barrier, inc=1, device_id=(sib, c), device_id_type=MESH)
    pl.semaphore_wait(barrier, 7)

    def remote(src, dst, send, recv, row, col):
        return pltpu.make_async_remote_copy(
            src, dst, send, recv, device_id=(row, col), device_id_type=MESH
        )

    def z_copy(d, slot):
        return remote(mine, xr.at[slab(slot)], zs.at[d], zr.at[d], r, (c + d) % 4)

    def chip_copy(d, slot):
        return remote(mine, xc.at[slab(slot)], gs.at[d], gr.at[d], 2 * chip_at(d) + core, c)

    def sib_copy(slot):
        return remote(mine, xc.at[slab(slot)], ss, sr, sib, c)

    def fwd_copy(d, slot):
        return remote(xc.at[slab(slot)], xc.at[slab(slot)], fs.at[d], fr.at[d], sib, c)

    def right(d, src):
        return remote(src, r_in.at[d], rs.at[d], rr.at[d], r, c + 1)

    def left(d, src):
        return remote(src, l_in.at[d], ls.at[d], lr.at[d], r, c - 1)

    def to_sib(d):
        return remote(
            m_ref.at[2 * chip_at(d) + 1 - core], from_sib.at[d], bs.at[d], br.at[d], sib, c
        )

    def to_chip(d):
        return remote(
            chip_out.at[d], chip_in.at[d], cs.at[d], cr.at[d], 2 * chip_at(d) + core, c
        )

    for d in (2, 1, 3):
        chip_copy(d, r).start()
        z_copy(d, c).start()
    sib_copy(r).start()
    own_r = pltpu.make_async_copy(mine, xr.at[slab(c)], own_sem.at[0])
    own_c = pltpu.make_async_copy(mine, xc.at[slab(r)], own_sem.at[1])
    own_r.start()
    own_c.start()

    def start_tiles(g, _):
        tile_copy(g).start()
        return 0

    lax.fori_loop(0, groups, start_tiles, 0)

    tile_row, tile_col = coords_v[0, 0], coords_v[1, 0]
    live = lax.broadcasted_iota(i32, (1, slots), 1) < count[0, 0]
    span = 4 * per_slab
    places = (tile_row % span, tile_col // span * per_slab + tile_col % per_slab)
    wide = slots * vecs
    spread = lax.broadcasted_iota(i32, (slots, wide), 1) // vecs
    spread = (spread == lax.broadcasted_iota(i32, (slots, wide), 0)).astype(f32).astype(bf16)
    across = lax.broadcasted_iota(i32, (vecs, wide), 1) % vecs
    same = across == lax.broadcasted_iota(i32, (vecs, wide), 0)
    for k in range(2):
        place = jnp.where(live, places[k], -1).astype(f32)
        place = jnp.broadcast_to(place, (vecs, slots)).astype(bf16)
        place = jnp.dot(place, spread, preferred_element_type=f32)
        keys[k] = jnp.where(same, place, -1.0)

    down = lax.broadcasted_iota(i32, (tile, tile), 0)
    over = lax.broadcasted_iota(i32, (tile, tile), 1)
    tri[0] = (down <= over).astype(f32).astype(bf16)
    tri[1] = (down < over).astype(f32).astype(bf16)

    def split_group(g, _):
        tile_copy(g).wait()
        for i in range(GROUP):
            s = g * GROUP + i
            gap = jnp.full((1, tile), coords[0, 0, 0, s] - coords[1, 0, 0, s], i32)
            off = jnp.minimum(gap * gap, 1).astype(f32).astype(bf16)
            stored = lower[s]
            upper[s] = stored * jnp.maximum(tri[0], off)
            lower[s] = stored * jnp.maximum(tri[1], off)
        return 0

    lax.fori_loop(0, groups, split_group, 0)

    for d in (2, 1, 3):
        slot = 2 * ((chip + 4 - d) % 4) + core
        chip_copy(d, slot).wait_recv()
        fwd_copy(d, slot).start()
    sib_copy(sib).wait_recv()
    own_c.wait()
    for d in (2, 1, 3):
        fwd_copy(d, 2 * ((chip + 4 - d) % 4) + 1 - core).wait_recv()

    def forward_group(g, _):
        outs = []
        for i in range(GROUP):
            s = g * GROUP + i
            col = coords[1, 0, 0, s]
            at = lax.div(col, span) * per_slab + lax.rem(col, per_slab)
            outs.append(
                lax.dot_general(
                    xc[at], upper[s], (((1,), (1,)), ((), ())),
                    preferred_element_type=f32,
                ).astype(bf16)
            )
        rows = pl.ds(pl.multiple_of(g * GROUP * vecs, GROUP * vecs), GROUP * vecs)
        made[rows, :] = jnp.concatenate(outs, axis=0)
        return 0

    def mirror_group(g, _):
        outs = []
        for i in range(GROUP):
            s = g * GROUP + i
            row = lax.rem(coords[0, 0, 0, s], span)
            outs.append(
                jnp.dot(xr[row], lower[s], preferred_element_type=f32).astype(bf16)
            )
        rows = pl.ds(pl.multiple_of(g * GROUP * vecs, GROUP * vecs), GROUP * vecs)
        made[rows, :] = jnp.concatenate(outs, axis=0)
        return 0

    def combine(k, owner, dst):
        def pick(p, _):
            rows = pl.ds(pl.multiple_of(p * vecs, vecs), vecs)
            wanted = (owner * per_slab + p).astype(f32)
            onehot[rows, :] = jnp.where(keys[k] == wanted, 1.0, 0.0).astype(bf16)
            return 0

        lax.fori_loop(0, per_slab, pick, 0, unroll=4)
        dst[owner] = jnp.dot(onehot[...], made[...], preferred_element_type=f32).astype(bf16)

    def add(dst, a, b):
        dst[...] = (a[...].astype(f32) + b[...].astype(f32)).astype(dst.dtype)

    def chain(at_right, d, at_left, e):
        @pl.when(c == at_right)
        def _():
            right(d, r_out.at[d]).wait_recv()
            add(r_out.at[d], f_ref.at[d], r_in.at[d])
            right(d, r_out.at[d]).start()

        @pl.when(c == at_left)
        def _():
            left(e, l_out.at[e]).wait_recv()
            add(l_out.at[e], f_ref.at[e], l_in.at[e])
            left(e, l_out.at[e]).start()

    lax.fori_loop(0, groups, forward_group, 0)

    def combine_f(d, _):
        combine(0, d, f_ref)
        return 0

    lax.fori_loop(0, 4, combine_f, 0)
    for i in range(3):

        @pl.when(c == 0)
        def _():
            right(3 - i, f_ref.at[3 - i]).start()

        @pl.when(c == 3)
        def _():
            left(i, f_ref.at[i]).start()

    own_r.wait()
    for d in (2, 1, 3):
        z_copy(d, (c + 4 - d) % 4).wait_recv()
    lax.fori_loop(0, groups, mirror_group, 0)
    chain(1, 3, 2, 0)

    def combine_theirs(j, _):
        combine(1, 2 * ((chip + 1 + j) % 4) + 1 - core, m_ref)
        to_sib((1 + j) % 4).start()
        return 0

    lax.fori_loop(0, 4, combine_theirs, 0)

    for d in (1, 2, 3):
        combine(1, 2 * chip_at(d) + core, m_ref)
        to_sib(d).wait_recv()
        add(chip_out.at[d], m_ref.at[2 * chip_at(d) + core], from_sib.at[d])
        to_chip(d).start()
        if d == 1:
            chain(1, 2, 2, 1)
    chain(2, 3, 1, 0)
    combine(1, r, m_ref)
    to_sib(0).wait_recv()
    for d in (1, 2, 3):
        to_chip(d).wait_recv()

    def rows_of(p):
        rows = pl.ds(pl.multiple_of(p * vecs, vecs), vecs)
        return rows, pl.ds(pl.multiple_of(p * tile, tile), tile)

    def total(p, _):
        rows, at = rows_of(p)
        out = f_ref[c, rows, :].astype(f32) + m_ref[r, rows, :].astype(f32)
        out = out + from_sib[0, rows, :].astype(f32)
        for d in (1, 2, 3):
            out = out + chip_in[d, rows, :].astype(f32)
        o_ref[:, at] = out
        return 0

    lax.fori_loop(0, per_slab, total, 0, unroll=4)

    def last(src):
        def body(p, _):
            rows, at = rows_of(p)
            o_ref[:, at] = o_ref[:, at] + src[c, rows, :].astype(f32)
            return 0

        lax.fori_loop(0, per_slab, body, 0, unroll=4)

    @pl.when(c > 0)
    def _():
        right(c, r_out.at[c]).wait_recv()
        last(r_in)

    @pl.when(c < 3)
    def _():
        left(c, l_out.at[c]).wait_recv()
        last(l_in)

    for d in (1, 2, 3):
        z_copy(d, c).wait_send()
        chip_copy(d, r).wait_send()
        fwd_copy(d, 2 * ((chip + 4 - d) % 4) + core).wait_send()
        to_chip(d).wait_send()
    sib_copy(r).wait_send()
    for d in range(4):
        to_sib(d).wait_send()
    for i in range(3):

        @pl.when(c < 3 - i)
        def _():
            right(3 - i, r_out.at[3 - i]).wait_send()

        @pl.when(c > i)
        def _():
            left(i, l_out.at[i]).wait_send()


def fused(tiles, tile_coords, tile_counts, x):
    slots, tile = tiles.shape[2], tiles.shape[-1]
    vecs, width = x.shape
    slab = width // tile
    rows = slab * vecs
    dma, bf16 = pltpu.SemaphoreType.DMA, jnp.bfloat16
    block = pltpu.VMEM((4, rows, tile), bf16)
    return pl.pallas_call(
        fused_kernel,
        out_shape=jax.ShapeDtypeStruct(x.shape, jnp.float32),
        in_specs=[
            pl.BlockSpec(memory_space=pltpu.SMEM),
            pl.BlockSpec(memory_space=pltpu.SMEM),
            pl.BlockSpec(memory_space=pltpu.VMEM),
            pl.BlockSpec(memory_space=pltpu.VMEM),
            pl.BlockSpec(memory_space=pl.ANY),
        ],
        out_specs=pl.BlockSpec(memory_space=pltpu.VMEM),
        scratch_shapes=[
            pltpu.VMEM((slab, vecs, tile), bf16),
            pltpu.VMEM((4 * slab, vecs, tile), bf16),
            pltpu.VMEM((8 * slab, vecs, tile), bf16),
            pltpu.VMEM((slots, tile, tile), bf16),
            pltpu.VMEM((slots, tile, tile), bf16),
            pltpu.VMEM((2, tile, tile), bf16),
            pltpu.VMEM((slots * vecs, tile), bf16),
            pltpu.VMEM((2, vecs, slots * vecs), jnp.float32),
            pltpu.VMEM((rows, slots * vecs), bf16),
            block,
            pltpu.VMEM((8, rows, tile), bf16),
            *[block] * 7,
            dma((slots // GROUP,)),
            dma((2,)),
            *[dma((4,))] * 4,
            *[dma] * 2,
            *[dma((4,))] * 10,
        ],
        compiler_params=pltpu.CompilerParams(
            collective_id=0, has_side_effects=True, vmem_limit_bytes=VMEM_LIMIT
        ),
        name="fused_product",
    )(tile_coords, tile_counts, tile_coords, x, tiles)


def apply_kernel(
    slots, tile, per_slab, n_cols, coords, count,
    t_ref, xr_ref, xc_ref, f_ref, m_ref, facc, macc,
):
    step = pl.program_id(0)
    group = t_ref.shape[2]

    @pl.when(step == 0)
    def _():
        facc[...] = jnp.zeros_like(facc)
        macc[...] = jnp.zeros_like(macc)

    def place(s):
        tile_row, tile_col = coords[s], coords[slots + s]
        local = tile_row % (per_slab * n_cols)
        row_at = (local // per_slab, pl.multiple_of(local % per_slab * tile, tile))
        col_at = (
            tile_col // (per_slab * n_cols), pl.multiple_of(tile_col % per_slab * tile, tile),
        )
        return row_at, col_at

    def run(masked):
        made = []
        for g in range(group):
            s = step * group + g
            (ro, rp), (co, cp) = place(s)
            x_row = xr_ref[ro, :, pl.ds(rp, tile)]
            x_col = xc_ref[co, :, pl.ds(cp, tile)]
            upper = lower = t_ref[0, 0, g]
            if masked:
                off = coords[s] != coords[slots + s]
                down = lax.broadcasted_iota(jnp.int32, (tile, tile), 0)
                down = jnp.where(off, -1, down)
                across = lax.broadcasted_iota(jnp.int32, (tile, tile), 1)
                stored = upper.astype(jnp.float32)
                upper = jnp.where(down <= across, stored, 0.0).astype(jnp.bfloat16)
                lower = jnp.where(down < across, stored, 0.0).astype(jnp.bfloat16)
            forward = lax.dot_general(
                x_col, upper, (((1,), (1,)), ((), ())), preferred_element_type=jnp.float32
            )
            mirror = lax.dot_general(
                x_row, lower, (((1,), (0,)), ((), ())), preferred_element_type=jnp.float32
            )
            if masked:
                live = s < count[0]
                forward = jnp.where(live, forward, 0.0)
                mirror = jnp.where(live, mirror, 0.0)
            made.append((forward, mirror))
        for g in range(group):
            (ro, rp), (co, cp) = place(step * group + g)
            forward, mirror = made[g]
            facc[ro, :, pl.ds(rp, tile)] += forward
            macc[co, :, pl.ds(cp, tile)] += mirror

    special = coords[step * group] == coords[slots + step * group]
    for g in range(1, group):
        s = step * group + g
        special = special | (coords[s] == coords[slots + s])
    special = special | (step * group + group > count[0])

    @pl.when(special)
    def _():
        run(True)

    @pl.when(jnp.logical_not(special))
    def _():
        run(False)

    @pl.when(step == pl.num_programs(0) - 1)
    def _():
        f_ref[...] = facc[...].astype(f_ref.dtype)
        m_ref[...] = macc[...].astype(m_ref.dtype)


def apply_tiles(tiles, coords, count, xr, xc, tile):
    slots = tiles.shape[2]
    group = GROUP if slots % GROUP == 0 else 1
    n_cols = xr.shape[0]
    per_slab = xr.shape[2] // tile
    whole = lambda a: pl.BlockSpec(a.shape, lambda i, *_: (0, 0, 0))
    return pl.pallas_call(
        functools.partial(apply_kernel, slots, tile, per_slab, n_cols),
        out_shape=(
            jax.ShapeDtypeStruct(xr.shape, jnp.bfloat16),
            jax.ShapeDtypeStruct(xc.shape, jnp.bfloat16),
        ),
        grid_spec=pltpu.PrefetchScalarGridSpec(
            num_scalar_prefetch=2,
            grid=(slots // group,),
            in_specs=[
                pl.BlockSpec((1, 1, group, tile, tile), lambda i, *_: (0, 0, i, 0, 0)),
                whole(xr),
                whole(xc),
            ],
            out_specs=(whole(xr), whole(xc)),
            scratch_shapes=[
                pltpu.VMEM(xr.shape, jnp.float32),
                pltpu.VMEM(xc.shape, jnp.float32),
            ],
        ),
        compiler_params=pltpu.CompilerParams(vmem_limit_bytes=VMEM_LIMIT),
        name="apply_tiles",
    )(coords, count, tiles, xr, xc)


def shards(n_rows, n_cols, tiles, tile_coords, tile_counts, vectors):
    tile = tiles.shape[-1]
    x = vectors.T
    if (n_rows, n_cols) == (8, 4):
        return fused(tiles, tile_coords, tile_counts, x).T
    coords, count = tile_coords.reshape(-1), tile_counts.reshape(-1)
    xr = lax.all_gather(x, "col", axis=0)
    xc = lax.all_gather(x, "row", axis=0)
    f, m = apply_tiles(tiles, coords, count, xr, xc, tile)
    f = lax.all_to_all(f, "col", 0, 0, tiled=True)
    m = lax.all_to_all(m, "row", 0, 0, tiled=True)
    return (jnp.sum(f.astype(jnp.float32), 0) + jnp.sum(m.astype(jnp.float32), 0)).T


def solution(mesh):
    in_specs = (
        P("row", "col", None, None, None),
        P(None, "row", "col", None),
        P("row", "col"),
        P(("row", "col"), None),
    )
    out_specs = P(("row", "col"), None)
    body = functools.partial(shards, mesh.shape["row"], mesh.shape["col"])
    return jax.shard_map(body, mesh=mesh, in_specs=in_specs, out_specs=out_specs, check_vma=False)
```

```python
import functools

import jax
import jax.numpy as jnp
from jax import lax
from jax.experimental import pallas as pl
from jax.experimental.pallas import tpu as pltpu
from jax.sharding import PartitionSpec as P

MESH = pl.DeviceIdType.MESH
VMEM_LIMIT = 48 * 1024 * 1024
GROUP = 8


def fused_kernel(
    coords, count, coords_v, x_ref, t_ref, o_ref,
    mine, xr, xc, upper, lower, tri, made, keys, onehot, f_ref, m_ref,
    from_sib, chip_out, chip_in, r_out, r_in, l_out, l_in,
    tile_sem, own_sem, zs, zr, gs, gr, ss, sr, fs, fr, bs, br, cs, cr, rs, rr, ls, lr,
):
    r, c = lax.axis_index("row"), lax.axis_index("col")
    chip, core = r // 2, r % 2
    sib = 2 * chip + 1 - core
    slots, tile = upper.shape[0], upper.shape[1]
    vecs, width = x_ref.shape
    per_slab = width // tile
    groups = slots // GROUP
    f32, bf16, i32 = jnp.float32, jnp.bfloat16, jnp.int32

    for p in range(per_slab):
        mine[p] = x_ref[:, p * tile : (p + 1) * tile]

    def slab(i):
        return pl.ds(i * per_slab, per_slab)

    def chip_at(d):
        return (chip + d) % 4

    def tile_copy(g):
        at = pl.ds(g * GROUP, GROUP)
        return pltpu.make_async_copy(t_ref.at[0, 0, at], lower.at[at], tile_sem.at[g])

    barrier = pltpu.get_barrier_semaphore()
    for d in range(1, 4):
        pl.semaphore_signal(barrier, inc=1, device_id=(r, (c + d) % 4), device_id_type=MESH)
        pl.semaphore_signal(
            barrier, inc=1, device_id=(2 * chip_at(d) + core, c), device_id_type=MESH
        )
    pl.semaphore_signal(barrier, inc=1, device_id=(sib, c), device_id_type=MESH)
    pl.semaphore_wait(barrier, 7)

    def remote(src, dst, send, recv, row, col):
        return pltpu.make_async_remote_copy(
            src, dst, send, recv, device_id=(row, col), device_id_type=MESH
        )

    def z_copy(d, slot):
        return remote(mine, xr.at[slab(slot)], zs.at[d], zr.at[d], r, (c + d) % 4)

    def chip_copy(d, slot):
        return remote(mine, xc.at[slab(slot)], gs.at[d], gr.at[d], 2 * chip_at(d) + core, c)

    def sib_copy(slot):
        return remote(mine, xc.at[slab(slot)], ss, sr, sib, c)

    def fwd_copy(d, slot):
        return remote(xc.at[slab(slot)], xc.at[slab(slot)], fs.at[d], fr.at[d], sib, c)

    def right(d, src):
        return remote(src, r_in.at[d], rs.at[d], rr.at[d], r, c + 1)

    def left(d, src):
        return remote(src, l_in.at[d], ls.at[d], lr.at[d], r, c - 1)

    def to_sib(d):
        return remote(
            m_ref.at[2 * chip_at(d) + 1 - core], from_sib.at[d], bs.at[d], br.at[d], sib, c
        )

    def to_chip(d):
        return remote(
            chip_out.at[d], chip_in.at[d], cs.at[d], cr.at[d], 2 * chip_at(d) + core, c
        )

    for d in (2, 1, 3):
        chip_copy(d, r).start()
        z_copy(d, c).start()
    sib_copy(r).start()
    own_r = pltpu.make_async_copy(mine, xr.at[slab(c)], own_sem.at[0])
    own_c = pltpu.make_async_copy(mine, xc.at[slab(r)], own_sem.at[1])
    own_r.start()
    own_c.start()

    def start_tiles(g, _):
        tile_copy(g).start()
        return 0

    lax.fori_loop(0, groups, start_tiles, 0)

    tile_row, tile_col = coords_v[0, 0], coords_v[1, 0]
    live = lax.broadcasted_iota(i32, (1, slots), 1) < count[0, 0]
    span = 4 * per_slab
    places = (tile_row % span, tile_col // span * per_slab + tile_col % per_slab)
    wide = slots * vecs
    spread = lax.broadcasted_iota(i32, (slots, wide), 1) // vecs
    spread = (spread == lax.broadcasted_iota(i32, (slots, wide), 0)).astype(f32).astype(bf16)
    across = lax.broadcasted_iota(i32, (vecs, wide), 1) % vecs
    same = across == lax.broadcasted_iota(i32, (vecs, wide), 0)
    for k in range(2):
        place = jnp.where(live, places[k], -1).astype(f32)
        place = jnp.broadcast_to(place, (vecs, slots)).astype(bf16)
        place = jnp.dot(place, spread, preferred_element_type=f32)
        keys[k] = jnp.where(same, place, -1.0)

    down = lax.broadcasted_iota(i32, (tile, tile), 0)
    over = lax.broadcasted_iota(i32, (tile, tile), 1)
    tri[0] = (down <= over).astype(f32).astype(bf16)
    tri[1] = (down < over).astype(f32).astype(bf16)

    def split_group(g, _):
        tile_copy(g).wait()
        for i in range(GROUP):
            s = g * GROUP + i
            gap = jnp.full((1, tile), coords[0, 0, 0, s] - coords[1, 0, 0, s], i32)
            off = jnp.minimum(gap * gap, 1).astype(f32).astype(bf16)
            stored = lower[s]
            upper[s] = stored * jnp.maximum(tri[0], off)
            lower[s] = stored * jnp.maximum(tri[1], off)
        return 0

    lax.fori_loop(0, groups, split_group, 0)

    for d in (2, 1, 3):
        slot = 2 * ((chip + 4 - d) % 4) + core
        chip_copy(d, slot).wait_recv()
        fwd_copy(d, slot).start()
    sib_copy(sib).wait_recv()
    own_c.wait()
    for d in (2, 1, 3):
        fwd_copy(d, 2 * ((chip + 4 - d) % 4) + 1 - core).wait_recv()

    def forward_group(g, _):
        outs = []
        for i in range(GROUP):
            s = g * GROUP + i
            col = coords[1, 0, 0, s]
            at = lax.div(col, span) * per_slab + lax.rem(col, per_slab)
            outs.append(
                lax.dot_general(
                    xc[at], upper[s], (((1,), (1,)), ((), ())),
                    preferred_element_type=f32,
                ).astype(bf16)
            )
        rows = pl.ds(pl.multiple_of(g * GROUP * vecs, GROUP * vecs), GROUP * vecs)
        made[rows, :] = jnp.concatenate(outs, axis=0)
        return 0

    def mirror_group(g, _):
        outs = []
        for i in range(GROUP):
            s = g * GROUP + i
            row = lax.rem(coords[0, 0, 0, s], span)
            outs.append(
                jnp.dot(xr[row], lower[s], preferred_element_type=f32).astype(bf16)
            )
        rows = pl.ds(pl.multiple_of(g * GROUP * vecs, GROUP * vecs), GROUP * vecs)
        made[rows, :] = jnp.concatenate(outs, axis=0)
        return 0

    def combine(k, owner, dst):
        def pick(p, _):
            rows = pl.ds(pl.multiple_of(p * vecs, vecs), vecs)
            wanted = (owner * per_slab + p).astype(f32)
            onehot[rows, :] = jnp.where(keys[k] == wanted, 1.0, 0.0).astype(bf16)
            return 0

        lax.fori_loop(0, per_slab, pick, 0, unroll=4)
        dst[owner] = jnp.dot(onehot[...], made[...], preferred_element_type=f32).astype(bf16)

    def add(dst, a, b):
        dst[...] = (a[...].astype(f32) + b[...].astype(f32)).astype(dst.dtype)

    def chain(at_right, d, at_left, e):
        @pl.when(c == at_right)
        def _():
            right(d, r_out.at[d]).wait_recv()
            add(r_out.at[d], f_ref.at[d], r_in.at[d])
            right(d, r_out.at[d]).start()

        @pl.when(c == at_left)
        def _():
            left(e, l_out.at[e]).wait_recv()
            add(l_out.at[e], f_ref.at[e], l_in.at[e])
            left(e, l_out.at[e]).start()

    lax.fori_loop(0, groups, forward_group, 0)

    half = c // 2
    for i in range(4):
        combine(0, (3 - i) * (1 - half) + i * half, f_ref)
        if i == 3:
            break

        @pl.when(c == 0)
        def _():
            right(3 - i, f_ref.at[3 - i]).start()

        @pl.when(c == 3)
        def _():
            left(i, f_ref.at[i]).start()

    own_r.wait()
    for d in (2, 1, 3):
        z_copy(d, (c + 4 - d) % 4).wait_recv()
    lax.fori_loop(0, groups, mirror_group, 0)
    chain(1, 3, 2, 0)

    def combine_theirs(j, _):
        combine(1, 2 * ((chip + 1 + j) % 4) + 1 - core, m_ref)
        to_sib((1 + j) % 4).start()
        return 0

    lax.fori_loop(0, 4, combine_theirs, 0)

    for d in (1, 2, 3):
        combine(1, 2 * chip_at(d) + core, m_ref)
        to_sib(d).wait_recv()
        add(chip_out.at[d], m_ref.at[2 * chip_at(d) + core], from_sib.at[d])
        to_chip(d).start()
        if d == 1:
            chain(1, 2, 2, 1)
    chain(2, 3, 1, 0)
    combine(1, r, m_ref)
    to_sib(0).wait_recv()
    for d in (1, 2, 3):
        to_chip(d).wait_recv()

    def rows_of(p):
        rows = pl.ds(pl.multiple_of(p * vecs, vecs), vecs)
        return rows, pl.ds(pl.multiple_of(p * tile, tile), tile)

    def total(p, _):
        rows, at = rows_of(p)
        out = f_ref[c, rows, :].astype(f32) + m_ref[r, rows, :].astype(f32)
        out = out + from_sib[0, rows, :].astype(f32)
        for d in (1, 2, 3):
            out = out + chip_in[d, rows, :].astype(f32)
        o_ref[:, at] = out
        return 0

    lax.fori_loop(0, per_slab, total, 0, unroll=4)

    def last(src):
        def body(p, _):
            rows, at = rows_of(p)
            o_ref[:, at] = o_ref[:, at] + src[c, rows, :].astype(f32)
            return 0

        lax.fori_loop(0, per_slab, body, 0, unroll=4)

    @pl.when(c > 0)
    def _():
        right(c, r_out.at[c]).wait_recv()
        last(r_in)

    @pl.when(c < 3)
    def _():
        left(c, l_out.at[c]).wait_recv()
        last(l_in)

    for d in (1, 2, 3):
        z_copy(d, c).wait_send()
        chip_copy(d, r).wait_send()
        fwd_copy(d, 2 * ((chip + 4 - d) % 4) + core).wait_send()
        to_chip(d).wait_send()
    sib_copy(r).wait_send()
    for d in range(4):
        to_sib(d).wait_send()
    for i in range(3):

        @pl.when(c < 3 - i)
        def _():
            right(3 - i, r_out.at[3 - i]).wait_send()

        @pl.when(c > i)
        def _():
            left(i, l_out.at[i]).wait_send()


def fused(tiles, tile_coords, tile_counts, x):
    slots, tile = tiles.shape[2], tiles.shape[-1]
    vecs, width = x.shape
    slab = width // tile
    rows = slab * vecs
    dma, bf16 = pltpu.SemaphoreType.DMA, jnp.bfloat16
    block = pltpu.VMEM((4, rows, tile), bf16)
    return pl.pallas_call(
        fused_kernel,
        out_shape=jax.ShapeDtypeStruct(x.shape, jnp.float32),
        in_specs=[
            pl.BlockSpec(memory_space=pltpu.SMEM),
            pl.BlockSpec(memory_space=pltpu.SMEM),
            pl.BlockSpec(memory_space=pltpu.VMEM),
            pl.BlockSpec(memory_space=pltpu.VMEM),
            pl.BlockSpec(memory_space=pl.ANY),
        ],
        out_specs=pl.BlockSpec(memory_space=pltpu.VMEM),
        scratch_shapes=[
            pltpu.VMEM((slab, vecs, tile), bf16),
            pltpu.VMEM((4 * slab, vecs, tile), bf16),
            pltpu.VMEM((8 * slab, vecs, tile), bf16),
            pltpu.VMEM((slots, tile, tile), bf16),
            pltpu.VMEM((slots, tile, tile), bf16),
            pltpu.VMEM((2, tile, tile), bf16),
            pltpu.VMEM((slots * vecs, tile), bf16),
            pltpu.VMEM((2, vecs, slots * vecs), jnp.float32),
            pltpu.VMEM((rows, slots * vecs), bf16),
            block,
            pltpu.VMEM((8, rows, tile), bf16),
            *[block] * 7,
            dma((slots // GROUP,)),
            dma((2,)),
            *[dma((4,))] * 4,
            *[dma] * 2,
            *[dma((4,))] * 10,
        ],
        compiler_params=pltpu.CompilerParams(
            collective_id=0, has_side_effects=True, vmem_limit_bytes=VMEM_LIMIT
        ),
        name="fused_product",
    )(tile_coords, tile_counts, tile_coords, x, tiles)


def apply_kernel(
    slots, tile, per_slab, n_cols, coords, count,
    t_ref, xr_ref, xc_ref, f_ref, m_ref, facc, macc,
):
    step = pl.program_id(0)
    group = t_ref.shape[2]

    @pl.when(step == 0)
    def _():
        facc[...] = jnp.zeros_like(facc)
        macc[...] = jnp.zeros_like(macc)

    def place(s):
        tile_row, tile_col = coords[s], coords[slots + s]
        local = tile_row % (per_slab * n_cols)
        row_at = (local // per_slab, pl.multiple_of(local % per_slab * tile, tile))
        col_at = (
            tile_col // (per_slab * n_cols), pl.multiple_of(tile_col % per_slab * tile, tile),
        )
        return row_at, col_at

    def run(masked):
        made = []
        for g in range(group):
            s = step * group + g
            (ro, rp), (co, cp) = place(s)
            x_row = xr_ref[ro, :, pl.ds(rp, tile)]
            x_col = xc_ref[co, :, pl.ds(cp, tile)]
            upper = lower = t_ref[0, 0, g]
            if masked:
                off = coords[s] != coords[slots + s]
                down = lax.broadcasted_iota(jnp.int32, (tile, tile), 0)
                down = jnp.where(off, -1, down)
                across = lax.broadcasted_iota(jnp.int32, (tile, tile), 1)
                stored = upper.astype(jnp.float32)
                upper = jnp.where(down <= across, stored, 0.0).astype(jnp.bfloat16)
                lower = jnp.where(down < across, stored, 0.0).astype(jnp.bfloat16)
            forward = lax.dot_general(
                x_col, upper, (((1,), (1,)), ((), ())), preferred_element_type=jnp.float32
            )
            mirror = lax.dot_general(
                x_row, lower, (((1,), (0,)), ((), ())), preferred_element_type=jnp.float32
            )
            if masked:
                live = s < count[0]
                forward = jnp.where(live, forward, 0.0)
                mirror = jnp.where(live, mirror, 0.0)
            made.append((forward, mirror))
        for g in range(group):
            (ro, rp), (co, cp) = place(step * group + g)
            forward, mirror = made[g]
            facc[ro, :, pl.ds(rp, tile)] += forward
            macc[co, :, pl.ds(cp, tile)] += mirror

    special = coords[step * group] == coords[slots + step * group]
    for g in range(1, group):
        s = step * group + g
        special = special | (coords[s] == coords[slots + s])
    special = special | (step * group + group > count[0])

    @pl.when(special)
    def _():
        run(True)

    @pl.when(jnp.logical_not(special))
    def _():
        run(False)

    @pl.when(step == pl.num_programs(0) - 1)
    def _():
        f_ref[...] = facc[...].astype(f_ref.dtype)
        m_ref[...] = macc[...].astype(m_ref.dtype)


def apply_tiles(tiles, coords, count, xr, xc, tile):
    slots = tiles.shape[2]
    group = GROUP if slots % GROUP == 0 else 1
    n_cols = xr.shape[0]
    per_slab = xr.shape[2] // tile
    whole = lambda a: pl.BlockSpec(a.shape, lambda i, *_: (0, 0, 0))
    return pl.pallas_call(
        functools.partial(apply_kernel, slots, tile, per_slab, n_cols),
        out_shape=(
            jax.ShapeDtypeStruct(xr.shape, jnp.bfloat16),
            jax.ShapeDtypeStruct(xc.shape, jnp.bfloat16),
        ),
        grid_spec=pltpu.PrefetchScalarGridSpec(
            num_scalar_prefetch=2,
            grid=(slots // group,),
            in_specs=[
                pl.BlockSpec((1, 1, group, tile, tile), lambda i, *_: (0, 0, i, 0, 0)),
                whole(xr),
                whole(xc),
            ],
            out_specs=(whole(xr), whole(xc)),
            scratch_shapes=[
                pltpu.VMEM(xr.shape, jnp.float32),
                pltpu.VMEM(xc.shape, jnp.float32),
            ],
        ),
        compiler_params=pltpu.CompilerParams(vmem_limit_bytes=VMEM_LIMIT),
        name="apply_tiles",
    )(coords, count, tiles, xr, xc)


def shards(n_rows, n_cols, tiles, tile_coords, tile_counts, vectors):
    tile = tiles.shape[-1]
    x = vectors.T
    if (n_rows, n_cols) == (8, 4):
        return fused(tiles, tile_coords, tile_counts, x).T
    coords, count = tile_coords.reshape(-1), tile_counts.reshape(-1)
    xr = lax.all_gather(x, "col", axis=0)
    xc = lax.all_gather(x, "row", axis=0)
    f, m = apply_tiles(tiles, coords, count, xr, xc, tile)
    f = lax.all_to_all(f, "col", 0, 0, tiled=True)
    m = lax.all_to_all(m, "row", 0, 0, tiled=True)
    return (jnp.sum(f.astype(jnp.float32), 0) + jnp.sum(m.astype(jnp.float32), 0)).T


def solution(mesh):
    in_specs = (
        P("row", "col", None, None, None),
        P(None, "row", "col", None),
        P("row", "col"),
        P(("row", "col"), None),
    )
    out_specs = P(("row", "col"), None)
    body = functools.partial(shards, mesh.shape["row"], mesh.shape["col"])
    return jax.shard_map(body, mesh=mesh, in_specs=in_specs, out_specs=out_specs, check_vma=False)
```
